128 devices in a mesh: pair: 8 (over z_lo, x), tile: 16 (over z_hi, y, core).
Axes of the slice: x: 4, y: 4, z: 4 (z_hi: 2, z_lo: 2; z = z_hi * 2 + z_lo), core: 2. Of those that a mesh axis runs over, the one named last changes fastest.
Arguments:
- wrapped: bfloat16 [512, 256, 512], P(None, ('tile', 'pair')), may hold values from -6 to 6
- projector: bfloat16 [512, 512], replicated, may hold values from -1 to 1
- cycles_down: int32 [256, 512], P('tile'), may hold values from -1 to 1
- cycles_across: int32 [256, 512], P('tile'), may hold values from -1 to 1
- weight_class: int32 [256, 512], P('tile'), may hold values from 0 to 3
Outputs:
- unwrapped: float32 [512, 256, 512], P('pair', 'tile')
- misfit: float32 [512, 256, 512], P(None, ('tile', 'pair'))
The draws below stay inside these ranges and needn't reach their ends.
All inputs are finite; a program needn't handle non-finite values.
Results may differ from the reference program's by a relative error of at most 0.0037.
Values may be sent and summed in bfloat16 or wider, within the bound.
No kernel may reach another device: no remote copies, remote signals or barrier semaphores. Data moves between devices by JAX's collectives and lax.ppermute only.
A program may use at most 64 MiB of HBM per device.

```python
import jax
import jax.numpy as jnp
from jax import lax

PAIRS = 512
STRIP = 16
COLS = 512
TEMP_ITERS = 6
SWEEPS = 8
ROWS = 256
N_PAIR = 8
N_TILE = 16


def draw_projector(key, part):
    entries = jax.random.normal(key, (PAIRS, PAIRS), jnp.float32)
    scaled = 0.6 * jnp.eye(PAIRS, dtype=jnp.float32) + 0.3 * entries / jnp.sqrt(jnp.float32(PAIRS))
    return scaled.astype(jnp.bfloat16)


def plant(values, key, least, top_value):
    dims = values.shape
    index_at = [jax.random.randint(jax.random.fold_in(key, axis), (), 0, dims[axis]) for axis in range(len(dims))]
    values = values.at[tuple(index_at)].set(least)
    longest = dims.index(max(dims))
    index_at[longest] = (index_at[longest] + 1) % dims[longest]
    return values.at[tuple(index_at)].set(top_value)


def block_levels(stream_key, dims, pieces, least, largest):
    def one(axis_at, shards_of):
        draws = jax.random.uniform(jax.random.fold_in(jax.random.fold_in(stream_key, 6), axis_at), (shards_of,), jnp.float32, least / len(pieces), largest / len(pieces))
        return jnp.repeat(jnp.exp(draws), dims[axis_at] // shards_of).reshape((-1,) + (1,) * (len(dims) - axis_at - 1))

    level = one(*pieces[0])
    for cut in pieces[1:]:
        level = level * one(*cut)
    return level


def normal_values(rng, shape, spread, bound, cuts=(), held_as=jnp.bfloat16):
    drawn = spread * jax.random.normal(rng, shape, jnp.float32)
    if cuts:
        drawn = drawn * block_levels(rng, shape, cuts, -0.22, 0.18)
    return jnp.clip(drawn, -bound, bound).astype(held_as)


def setup_inputs(seed: int = 0) -> dict:
    key_of = jax.random.split(jax.random.key(seed), 6)
    wrapped = normal_values(key_of[0], (PAIRS, ROWS, COLS), 1.0, 6.0, ((1, 128),))
    projector = draw_projector(jax.random.fold_in(key_of[5], 71), 0)
    cycles_down = plant(jax.random.randint(key_of[2], (ROWS, COLS), -1, 2), jax.random.fold_in(key_of[2], 1), -1, 1).astype(jnp.int32)
    cycles_across = plant(jax.random.randint(key_of[3], (ROWS, COLS), -1, 2), jax.random.fold_in(key_of[3], 1), -1, 1).astype(jnp.int32)
    weight_class = plant(jax.random.randint(key_of[4], (ROWS, COLS), 0, 4), jax.random.fold_in(key_of[4], 1), 0, 3).astype(jnp.int32)
    return {"wrapped": wrapped, "projector": projector, "cycles_down": cycles_down, "cycles_across": cycles_across, "weight_class": weight_class}


SHRINK = 0.5
DUAL_STEP = 0.35
PRIMAL_STEP = 0.35
FIDELITY = 0.5
LEVELS = (0.25, 0.5, 1.0, 2.0)


def weights_of(classes):
    limits = jnp.zeros(classes.shape, jnp.float32)
    for number, weight_level in enumerate(LEVELS):
        limits = limits + jnp.where(classes == number, weight_level, 0.0)
    return limits


def down_step(values, below_row, row_valid):
    following = jnp.concatenate([values[:, 1:], below_row], axis=1)
    return jnp.where(row_valid, following - values, 0.0)


def across_step(values, col_valid):
    following = jnp.concatenate([values[:, :, 1:], jnp.zeros_like(values[:, :, :1])], axis=2)
    return jnp.where(col_valid, following - values, 0.0)


def temporal_section(stripe, projector):
    phases = stripe.astype(jnp.float32)
    misfit = jnp.zeros(phases.shape, jnp.float32)
    multiplier = jnp.zeros(phases.shape, jnp.float32)
    mapped = phases
    for iteration in range(TEMP_ITERS):
        blended = (phases + misfit - multiplier).astype(jnp.bfloat16)
        mapped = jnp.dot(projector, blended.reshape(PAIRS, -1), preferred_element_type=jnp.float32).reshape(phases.shape)
        excess = mapped - phases + multiplier
        misfit = excess - jnp.clip(excess, -SHRINK, SHRINK)
        multiplier = excess - misfit
    return mapped.astype(jnp.bfloat16), misfit


def spatial_section(estimate, cycles_down, cycles_across, weight_class):
    anchor = estimate.astype(jnp.float32)
    row_valid = (jnp.arange(ROWS) < ROWS - 1)[:, None]
    col_valid = jnp.arange(COLS) < COLS - 1
    zero_row = jnp.zeros_like(anchor[:, :1])
    zero_col = jnp.zeros_like(anchor[:, :, :1])
    target_down = down_step(anchor, zero_row, row_valid) + jnp.where(row_valid, cycles_down.astype(jnp.float32), 0.0)
    target_across = across_step(anchor, col_valid) + jnp.where(col_valid, cycles_across.astype(jnp.float32), 0.0)
    limits = weights_of(weight_class)
    primal = anchor
    primal_bar = anchor
    dual_down = jnp.zeros_like(anchor)
    dual_across = jnp.zeros_like(anchor)
    for sweep_index in range(SWEEPS):
        dual_down = jnp.clip(dual_down + DUAL_STEP * (down_step(primal_bar, zero_row, row_valid) - target_down), -limits, limits)
        dual_across = jnp.clip(dual_across + DUAL_STEP * (across_step(primal_bar, col_valid) - target_across), -limits, limits)
        diverge = dual_down - jnp.concatenate([zero_row, dual_down[:, :-1]], axis=1)
        diverge = diverge + dual_across - jnp.concatenate([zero_col, dual_across[:, :, :-1]], axis=2)
        updated = (primal + PRIMAL_STEP * diverge + PRIMAL_STEP * FIDELITY * anchor) / (1.0 + PRIMAL_STEP * FIDELITY)
        primal_bar = 2.0 * updated - primal
        primal = updated
    return primal


def reference(wrapped, projector, cycles_down, cycles_across, weight_class):
    stacked = wrapped.reshape(PAIRS, N_TILE, STRIP, COLS).transpose(1, 0, 2, 3)

    def temporal_piece(stripe):
        return temporal_section(stripe, projector)

    estimate, misfit = lax.map(temporal_piece, stacked)
    estimate = estimate.transpose(1, 0, 2, 3).reshape(PAIRS, ROWS, COLS)
    misfit = misfit.transpose(1, 0, 2, 3).reshape(PAIRS, ROWS, COLS)
    grouped = estimate.reshape(N_PAIR, PAIRS // N_PAIR, ROWS, COLS)

    def spatial_piece(group):
        return spatial_section(group, cycles_down, cycles_across, weight_class)

    unwrapped = lax.map(spatial_piece, grouped).reshape(PAIRS, ROWS, COLS)
    return unwrapped, misfit
```

```python
import functools

import jax
import jax.numpy as jnp
from jax import lax
from jax.experimental import pallas as pl
from jax.experimental.pallas import tpu as pltpu
from jax.sharding import PartitionSpec as P

TEMP_ITERS = 6
SWEEPS = 8


SHRINK = 0.5
DUAL_STEP = 0.35
PRIMAL_STEP = 0.35
FIDELITY = 0.5
LEVELS = (0.25, 0.5, 1.0, 2.0)

HALO = 8
LANES = 128
VMEM_LIMIT = 40 * 2**20


def clip(value, bound):
    return jnp.minimum(jnp.maximum(value, -bound), bound)


def temporal_kernel(wrapped_ref, projector_ref, estimate_ref, misfit_ref, phases_ref, multiplier_ref):
    pairs = projector_ref.shape[0]
    per_pair = wrapped_ref.shape[0] // pairs
    peers, rows, group, _ = estimate_ref.shape
    pieces, _, width = multiplier_ref.shape
    wide = width // LANES

    def parts_of(piece):
        return range(piece * wide, (piece + 1) * wide)

    phases_ref[...] = wrapped_ref[...].astype(jnp.float32)
    projector = projector_ref[...]

    def phases_of(piece):
        return jnp.concatenate([phases_ref[pl.ds(k, pairs, stride=per_pair), :] for k in parts_of(piece)], axis=1)

    blended = [phases_of(piece).astype(jnp.bfloat16) for piece in range(pieces)]
    for iteration in range(TEMP_ITERS):
        for piece in range(pieces):
            mapped = jnp.dot(projector, blended[piece], preferred_element_type=jnp.float32)
            carried = mapped if iteration == 0 else mapped + multiplier_ref[piece]
            excess = carried - phases_of(piece)
            multiplier = clip(excess, SHRINK)
            if iteration < TEMP_ITERS - 1:
                multiplier_ref[piece] = multiplier
                blended[piece] = (carried - 2.0 * multiplier).astype(jnp.bfloat16)
                continue
            misfit = excess - multiplier
            estimate = mapped.astype(jnp.bfloat16)
            for at, k in enumerate(parts_of(piece)):
                columns = slice(at * LANES, (at + 1) * LANES)
                misfit_ref[pl.ds(k, pairs, stride=per_pair), :] = misfit[:, columns]
                tile, row = divmod(k, rows)
                for peer in range(peers):
                    estimate_ref[peer, row, :, tile * LANES : (tile + 1) * LANES] = estimate[
                        peer * group : (peer + 1) * group, columns
                    ]


def temporal_section(wrapped, projector, peers):
    pairs, rows, columns = wrapped.shape
    tiles = columns // LANES
    flat = wrapped.reshape(pairs, rows, tiles, LANES).transpose(0, 2, 1, 3).reshape(-1, LANES)
    in_vmem = pl.BlockSpec(memory_space=pltpu.VMEM)
    width = 2 * LANES
    pieces = rows * columns // width
    estimate, misfit = pl.pallas_call(
        temporal_kernel,
        out_shape=(
            jax.ShapeDtypeStruct((peers, rows, pairs // peers, columns), jnp.bfloat16),
            jax.ShapeDtypeStruct(flat.shape, jnp.float32),
        ),
        in_specs=[in_vmem, in_vmem],
        out_specs=(in_vmem, in_vmem),
        scratch_shapes=[pltpu.VMEM(flat.shape, jnp.float32), pltpu.VMEM((pieces, pairs, width), jnp.float32)],
        compiler_params=pltpu.CompilerParams(vmem_limit_bytes=VMEM_LIMIT),
        cost_estimate=pl.CostEstimate(
            flops=2 * TEMP_ITERS * pairs * pairs * rows * columns, bytes_accessed=4 * 2**20, transcendentals=0
        ),
    )(flat, projector)
    misfit = misfit.reshape(pairs, tiles, rows, LANES).transpose(0, 2, 1, 3).reshape(pairs, rows, columns)
    return estimate, misfit


def deviation_kernel(above_ref, own_ref, below_ref, deviation_ref):
    def extended(at):
        return jnp.concatenate([ref[at] for ref in (above_ref, own_ref, below_ref)], axis=0).astype(jnp.float32)

    cycles_down, cycles_across, classes = extended(0), extended(1), extended(2)
    rows, columns = classes.shape
    limits = jnp.zeros(classes.shape, jnp.float32)
    for number, level in enumerate(LEVELS):
        limits = limits + jnp.where(classes == number + 1, level, 0.0)
    is_last = lax.broadcasted_iota(jnp.int32, classes.shape, 1) == columns - 1
    limits_across = jnp.where(is_last, 0.0, limits)
    limits_down = jnp.where(pltpu.roll(classes, rows - 1, 0) == 0, 0.0, limits)
    step_down, step_across = DUAL_STEP * cycles_down, DUAL_STEP * cycles_across
    shrink = 1.0 / (1.0 + PRIMAL_STEP * FIDELITY)

    zero = jnp.zeros(classes.shape, jnp.float32)
    deviation, deviation_bar, dual_down, dual_across = zero, zero, zero, zero
    for _ in range(SWEEPS):
        down = pltpu.roll(deviation_bar, rows - 1, 0) - deviation_bar
        across = pltpu.roll(deviation_bar, columns - 1, 1) - deviation_bar
        dual_down = clip(dual_down + DUAL_STEP * down - step_down, limits_down)
        dual_across = clip(dual_across + DUAL_STEP * across - step_across, limits_across)
        diverge = dual_down - pltpu.roll(dual_down, 1, 0) + dual_across - pltpu.roll(dual_across, 1, 1)
        updated = (deviation + PRIMAL_STEP * diverge) * shrink
        deviation_bar = 2.0 * updated - deviation
        deviation = updated
    deviation_ref[...] = deviation[HALO : HALO + deviation_ref.shape[0]]


def shifted(value, axis, by):
    peers = lax.axis_size(axis)
    pairs = [(i, i + by) for i in range(peers) if 0 <= i + by < peers]
    return lax.ppermute(value, axis, pairs)


def deviation_section(cycles_down, cycles_across, weight_class):
    own = jnp.stack([cycles_down, cycles_across, weight_class + 1])
    above = shifted(own[:, -HALO:], "tile", 1)
    below = shifted(own[:, :HALO], "tile", -1)
    in_vmem = pl.BlockSpec(memory_space=pltpu.VMEM)
    return pl.pallas_call(
        deviation_kernel,
        out_shape=jax.ShapeDtypeStruct(cycles_down.shape, jnp.float32),
        in_specs=[in_vmem] * 3,
        out_specs=in_vmem,
        compiler_params=pltpu.CompilerParams(vmem_limit_bytes=8 * 2**20),
        cost_estimate=pl.CostEstimate(flops=4 * 2**20, bytes_accessed=2**18, transcendentals=0),
    )(above, own, below)


def combine_kernel(order_ref, estimate_ref, deviation_ref, unwrapped_ref):
    rows, group, columns = estimate_ref.shape
    turned = jnp.dot(
        order_ref[...], estimate_ref[...].reshape(rows * group, columns), preferred_element_type=jnp.float32
    )
    unwrapped_ref[...] = turned.reshape(group, rows, columns) + deviation_ref[...][None]


def combine(estimate, deviation):
    rows, pairs, columns = estimate.shape
    group = 16
    size = rows * group
    place = jnp.arange(size)
    source = place % rows * group + place // rows
    order = (source[:, None] == place[None]).astype(jnp.bfloat16)
    return pl.pallas_call(
        combine_kernel,
        grid=(pairs // group,),
        out_shape=jax.ShapeDtypeStruct((pairs, rows, columns), jnp.float32),
        in_specs=[
            pl.BlockSpec((size, size), lambda i: (0, 0)),
            pl.BlockSpec((rows, group, columns), lambda i: (0, i, 0)),
            pl.BlockSpec((rows, columns), lambda i: (0, 0)),
        ],
        out_specs=pl.BlockSpec((group, rows, columns), lambda i: (i, 0, 0)),
        compiler_params=pltpu.CompilerParams(vmem_limit_bytes=16 * 2**20),
    )(order, estimate, deviation)


def per_device(wrapped, projector, cycles_down, cycles_across, weight_class):
    estimate, misfit = temporal_section(wrapped, projector, lax.axis_size("pair"))
    moved = lax.all_to_all(estimate, "pair", split_axis=0, concat_axis=0, tiled=True)
    deviation = deviation_section(cycles_down, cycles_across, weight_class)
    peers, rows, group, columns = moved.shape
    unwrapped = combine(moved.reshape(peers * rows, group, columns), deviation)
    return unwrapped, misfit


def solution(mesh):
    placed = (
        P(None, ("tile", "pair"), None),
        P(),
        P("tile", None),
        P("tile", None),
        P("tile", None),
    )
    return jax.shard_map(
        per_device,
        mesh=mesh,
        in_specs=placed,
        out_specs=(P("pair", "tile", None), P(None, ("tile", "pair"), None)),
        check_vma=False,
    )
```

```python
import functools

import jax
import jax.numpy as jnp
from jax import lax
from jax.experimental import pallas as pl
from jax.experimental.pallas import tpu as pltpu
from jax.sharding import PartitionSpec as P

TEMP_ITERS = 6
SWEEPS = 8


SHRINK = 0.5
DUAL_STEP = 0.35
PRIMAL_STEP = 0.35
FIDELITY = 0.5
LEVELS = (0.25, 0.5, 1.0, 2.0)

HALO = 8
LANES = 128
VMEM_LIMIT = 58 * 2**20


def clip(value, bound):
    return jnp.minimum(jnp.maximum(value, -bound), bound)


def temporal_kernel(
    wrapped_hbm,
    projector_hbm,
    estimate_hbm,
    misfit_ref,
    wrapped_ref,
    projector_ref,
    spread_ref,
    phases_ref,
    multiplier_ref,
    blended_ref,
    estimate_ref,
    in_sems,
    out_sems,
):
    pairs = projector_ref.shape[0]
    per_pair = wrapped_ref.shape[0] // pairs
    peers, rows, group, _ = estimate_ref.shape
    pieces, _, width = multiplier_ref.shape
    wide = width // LANES
    loads = in_sems.shape[0] - 1
    load_rows = wrapped_ref.shape[0] // loads
    load_pairs = pairs // loads

    def parts_of(piece):
        return enumerate(range(piece * wide, (piece + 1) * wide))

    copies = []
    for load in range(loads):
        part = pl.ds(load * load_rows, load_rows)
        copies.append(pltpu.make_async_copy(wrapped_hbm.at[part], wrapped_ref.at[part], in_sems.at[load]))
    copies.append(pltpu.make_async_copy(projector_hbm, projector_ref, in_sems.at[loads]))
    for copy in copies:
        copy.start()
    for load in range(loads):
        copies[load].wait()
        first = load * load_rows
        spread_ref[first : first + load_rows, :] = wrapped_ref[first : first + load_rows, :].astype(jnp.float32)
        at_pairs = slice(load * load_pairs, (load + 1) * load_pairs)
        for piece in range(pieces):
            for at, k in parts_of(piece):
                columns = slice(at * LANES, (at + 1) * LANES)
                phases = spread_ref[pl.ds(first + k, load_pairs, stride=per_pair), :]
                phases_ref[piece, at_pairs, columns] = phases
                blended_ref[piece, at_pairs, columns] = phases.astype(jnp.bfloat16)
    copies[loads].wait()

    sent = []
    for iteration in range(TEMP_ITERS):
        for piece in range(pieces):
            mapped = jnp.dot(projector_ref[...], blended_ref[piece], preferred_element_type=jnp.float32)
            carried = mapped if iteration == 0 else mapped + multiplier_ref[piece]
            excess = carried - phases_ref[piece]
            multiplier = clip(excess, SHRINK)
            if iteration < TEMP_ITERS - 1:
                multiplier_ref[piece] = multiplier
                blended_ref[piece] = (carried - 2.0 * multiplier).astype(jnp.bfloat16)
                continue
            misfit = excess - multiplier
            estimate = mapped.astype(jnp.bfloat16)
            for at, k in parts_of(piece):
                columns = slice(at * LANES, (at + 1) * LANES)
                tile, row = divmod(k, rows)
                for peer in range(peers):
                    estimate_ref[peer, row, :, tile * LANES : (tile + 1) * LANES] = estimate[
                        peer * group : (peer + 1) * group, columns
                    ]
            done = pl.ds(piece * width // rows, width // rows)
            copy = pltpu.make_async_copy(
                estimate_ref.at[:, :, :, done], estimate_hbm.at[:, :, :, done], out_sems.at[piece]
            )
            copy.start()
            sent.append(copy)
            for at, k in parts_of(piece):
                misfit_ref[pl.ds(k, pairs, stride=per_pair), :] = misfit[:, at * LANES : (at + 1) * LANES]
    for copy in sent:
        copy.wait()


def temporal_section(wrapped, projector, peers):
    pairs, rows, columns = wrapped.shape
    tiles = columns // LANES
    flat = wrapped.reshape(pairs, rows, tiles, LANES).transpose(0, 2, 1, 3).reshape(-1, LANES)
    anywhere = pl.BlockSpec(memory_space=pl.ANY)
    width = 2 * LANES
    pieces = rows * columns // width
    loads = 4
    sent = (peers, rows, pairs // peers, columns)
    estimate, misfit = pl.pallas_call(
        temporal_kernel,
        out_shape=(jax.ShapeDtypeStruct(sent, jnp.bfloat16), pltpu.VMEM(flat.shape, jnp.float32)),
        in_specs=[anywhere, anywhere],
        out_specs=(anywhere, pl.BlockSpec(memory_space=pltpu.VMEM)),
        scratch_shapes=[
            pltpu.VMEM(flat.shape, jnp.bfloat16),
            pltpu.VMEM(projector.shape, jnp.bfloat16),
            pltpu.VMEM(flat.shape, jnp.float32),
            pltpu.VMEM((pieces, pairs, width), jnp.float32),
            pltpu.VMEM((pieces, pairs, width), jnp.float32),
            pltpu.VMEM((pieces, pairs, width), jnp.bfloat16),
            pltpu.VMEM(sent, jnp.bfloat16),
            pltpu.SemaphoreType.DMA((loads + 1,)),
            pltpu.SemaphoreType.DMA((pieces,)),
        ],
        compiler_params=pltpu.CompilerParams(vmem_limit_bytes=VMEM_LIMIT),
        cost_estimate=pl.CostEstimate(
            flops=2 * TEMP_ITERS * pairs * pairs * rows * columns, bytes_accessed=4 * 2**20, transcendentals=0
        ),
    )(flat, projector)
    misfit = misfit.reshape(pairs, tiles, rows, LANES).transpose(0, 2, 1, 3).reshape(pairs, rows, columns)
    return estimate, misfit


def deviation_kernel(above_ref, own_ref, below_ref, deviation_ref):
    def extended(at):
        return jnp.concatenate([ref[at] for ref in (above_ref, own_ref, below_ref)], axis=0).astype(jnp.float32)

    cycles_down, cycles_across, classes = extended(0), extended(1), extended(2)
    rows, columns = classes.shape
    limits = jnp.zeros(classes.shape, jnp.float32)
    for number, level in enumerate(LEVELS):
        limits = limits + jnp.where(classes == number + 1, level, 0.0)
    is_last = lax.broadcasted_iota(jnp.int32, classes.shape, 1) == columns - 1
    limits_across = jnp.where(is_last, 0.0, limits)
    limits_down = jnp.where(pltpu.roll(classes, rows - 1, 0) == 0, 0.0, limits)
    step_down, step_across = DUAL_STEP * cycles_down, DUAL_STEP * cycles_across
    shrink = 1.0 / (1.0 + PRIMAL_STEP * FIDELITY)

    zero = jnp.zeros(classes.shape, jnp.float32)
    deviation, deviation_bar, dual_down, dual_across = zero, zero, zero, zero
    for _ in range(SWEEPS):
        down = pltpu.roll(deviation_bar, rows - 1, 0) - deviation_bar
        across = pltpu.roll(deviation_bar, columns - 1, 1) - deviation_bar
        dual_down = clip(dual_down + DUAL_STEP * down - step_down, limits_down)
        dual_across = clip(dual_across + DUAL_STEP * across - step_across, limits_across)
        diverge = dual_down - pltpu.roll(dual_down, 1, 0) + dual_across - pltpu.roll(dual_across, 1, 1)
        updated = (deviation + PRIMAL_STEP * diverge) * shrink
        deviation_bar = 2.0 * updated - deviation
        deviation = updated
    deviation_ref[...] = deviation[HALO : HALO + deviation_ref.shape[0]]


def shifted(value, axis, by):
    peers = lax.axis_size(axis)
    pairs = [(i, i + by) for i in range(peers) if 0 <= i + by < peers]
    return lax.ppermute(value, axis, pairs)


def deviation_section(cycles_down, cycles_across, weight_class):
    own = jnp.stack([cycles_down, cycles_across, weight_class + 1])
    above = shifted(own[:, -HALO:], "tile", 1)
    below = shifted(own[:, :HALO], "tile", -1)
    in_vmem = pl.BlockSpec(memory_space=pltpu.VMEM)
    return pl.pallas_call(
        deviation_kernel,
        out_shape=jax.ShapeDtypeStruct(cycles_down.shape, jnp.float32),
        in_specs=[in_vmem] * 3,
        out_specs=in_vmem,
        compiler_params=pltpu.CompilerParams(vmem_limit_bytes=8 * 2**20),
        cost_estimate=pl.CostEstimate(flops=4 * 2**20, bytes_accessed=2**18, transcendentals=0),
    )(above, own, below)


def combine_kernel(order_ref, estimate_ref, deviation_ref, unwrapped_hbm, unwrapped_ref, sems):
    rows, pairs, columns = estimate_ref.shape
    group = order_ref.shape[0] // rows
    sent = []
    for at in range(pairs // group):
        part = pl.ds(at * group, group)
        turned = jnp.dot(
            order_ref[...],
            estimate_ref[:, part, :].reshape(rows * group, columns),
            preferred_element_type=jnp.float32,
        )
        unwrapped_ref[part] = turned.reshape(group, rows, columns) + deviation_ref[...][None]
        copy = pltpu.make_async_copy(unwrapped_ref.at[part], unwrapped_hbm.at[part], sems.at[at])
        copy.start()
        sent.append(copy)
    for copy in sent:
        copy.wait()


def combine(estimate, deviation):
    rows, pairs, columns = estimate.shape
    group = 16
    size = rows * group
    place = jnp.arange(size)
    source = place % rows * group + place // rows
    order = (source[:, None] == place[None]).astype(jnp.bfloat16)
    out = jax.ShapeDtypeStruct((pairs, rows, columns), jnp.float32)
    return pl.pallas_call(
        combine_kernel,
        out_shape=out,
        in_specs=[pl.BlockSpec(memory_space=pltpu.VMEM)] * 3,
        out_specs=pl.BlockSpec(memory_space=pl.ANY),
        scratch_shapes=[pltpu.VMEM(out.shape, out.dtype), pltpu.SemaphoreType.DMA((pairs // group,))],
        compiler_params=pltpu.CompilerParams(vmem_limit_bytes=16 * 2**20),
    )(order, estimate, deviation)


def per_device(wrapped, projector, cycles_down, cycles_across, weight_class):
    estimate, misfit = temporal_section(wrapped, projector, lax.axis_size("pair"))
    moved = lax.all_to_all(estimate, "pair", split_axis=0, concat_axis=0, tiled=True)
    deviation = deviation_section(cycles_down, cycles_across, weight_class)
    peers, rows, group, columns = moved.shape
    unwrapped = combine(moved.reshape(peers * rows, group, columns), deviation)
    return unwrapped, misfit


def solution(mesh):
    placed = (
        P(None, ("tile", "pair"), None),
        P(),
        P("tile", None),
        P("tile", None),
        P("tile", None),
    )
    return jax.shard_map(
        per_device,
        mesh=mesh,
        in_specs=placed,
        out_specs=(P("pair", "tile", None), P(None, ("tile", "pair"), None)),
        check_vma=False,
    )
```

```python
import functools

import jax
import jax.numpy as jnp
from jax import lax
from jax.experimental import pallas as pl
from jax.experimental.pallas import tpu as pltpu
from jax.sharding import PartitionSpec as P

TEMP_ITERS = 6
SWEEPS = 8


SHRINK = 0.5
DUAL_STEP = 0.35
PRIMAL_STEP = 0.35
FIDELITY = 0.5
LEVELS = (0.25, 0.5, 1.0, 2.0)

HALO = 8
LANES = 128
VMEM_LIMIT = 58 * 2**20


def clip(value, bound):
    return jnp.minimum(jnp.maximum(value, -bound), bound)


def temporal_kernel(
    wrapped_hbm,
    projector_hbm,
    estimate_hbm,
    misfit_ref,
    wrapped_ref,
    projector_ref,
    spread_ref,
    phases_ref,
    multiplier_ref,
    blended_ref,
    estimate_ref,
    in_sems,
    out_sems,
):
    pairs = projector_ref.shape[0]
    per_pair = wrapped_ref.shape[0] // pairs
    peers, rows, group, _ = estimate_ref.shape
    pieces, _, width = multiplier_ref.shape
    wide = width // LANES
    loads = in_sems.shape[0] - 1
    load_rows = wrapped_ref.shape[0] // loads
    load_pairs = pairs // loads

    def parts_of(piece):
        return enumerate(range(piece * wide, (piece + 1) * wide))

    copies = []
    for load in range(loads):
        part = pl.ds(load * load_rows, load_rows)
        copies.append(pltpu.make_async_copy(wrapped_hbm.at[part], wrapped_ref.at[part], in_sems.at[load]))
    copies.append(pltpu.make_async_copy(projector_hbm, projector_ref, in_sems.at[loads]))
    for copy in copies:
        copy.start()
    for load in range(loads):
        copies[load].wait()
        first = load * load_rows
        spread_ref[first : first + load_rows, :] = wrapped_ref[first : first + load_rows, :].astype(jnp.float32)
        at_pairs = slice(load * load_pairs, (load + 1) * load_pairs)
        for piece in range(pieces):
            for at, k in parts_of(piece):
                columns = slice(at * LANES, (at + 1) * LANES)
                phases = spread_ref[pl.ds(first + k, load_pairs, stride=per_pair), :]
                phases_ref[piece, at_pairs, columns] = phases
                blended_ref[piece, at_pairs, columns] = phases.astype(jnp.bfloat16)
    copies[loads].wait()

    half = pairs // 2
    sent = []
    for iteration in range(TEMP_ITERS):
        for piece in range(pieces):
            blended, following = blended_ref[piece], []
            for begin in (0, half):
                part = slice(begin, begin + half)
                mapped = jnp.dot(projector_ref[part, :], blended, preferred_element_type=jnp.float32)
                carried = mapped if iteration == 0 else mapped + multiplier_ref[piece, part]
                excess = carried - phases_ref[piece, part]
                multiplier = clip(excess, SHRINK)
                if iteration < TEMP_ITERS - 1:
                    multiplier_ref[piece, part] = multiplier
                    following.append((carried - 2.0 * multiplier).astype(jnp.bfloat16))
                    continue
                misfit = excess - multiplier
                estimate = mapped.astype(jnp.bfloat16)
                for at, k in parts_of(piece):
                    columns = slice(at * LANES, (at + 1) * LANES)
                    tile, row = divmod(k, rows)
                    for block in range(half // group):
                        estimate_ref[begin // group + block, row, :, tile * LANES : (tile + 1) * LANES] = estimate[
                            block * group : (block + 1) * group, columns
                        ]
                    misfit_ref[pl.ds(begin * per_pair + k, half, stride=per_pair), :] = misfit[:, columns]
            for begin, value in zip((0, half), following):
                blended_ref[piece, begin : begin + half] = value
            if iteration == TEMP_ITERS - 1:
                done = pl.ds(piece * width // rows, width // rows)
                copy = pltpu.make_async_copy(
                    estimate_ref.at[:, :, :, done], estimate_hbm.at[:, :, :, done], out_sems.at[piece]
                )
                copy.start()
                sent.append(copy)
    for copy in sent:
        copy.wait()


def temporal_section(wrapped, projector, peers):
    pairs, rows, columns = wrapped.shape
    tiles = columns // LANES
    flat = wrapped.reshape(pairs, rows, tiles, LANES).transpose(0, 2, 1, 3).reshape(-1, LANES)
    anywhere = pl.BlockSpec(memory_space=pl.ANY)
    width = 2 * LANES
    pieces = rows * columns // width
    loads = 4
    sent = (peers, rows, pairs // peers, columns)
    estimate, misfit = pl.pallas_call(
        temporal_kernel,
        out_shape=(jax.ShapeDtypeStruct(sent, jnp.bfloat16), pltpu.VMEM(flat.shape, jnp.float32)),
        in_specs=[anywhere, anywhere],
        out_specs=(anywhere, pl.BlockSpec(memory_space=pltpu.VMEM)),
        scratch_shapes=[
            pltpu.VMEM(flat.shape, jnp.bfloat16),
            pltpu.VMEM(projector.shape, jnp.bfloat16),
            pltpu.VMEM(flat.shape, jnp.float32),
            pltpu.VMEM((pieces, pairs, width), jnp.float32),
            pltpu.VMEM((pieces, pairs, width), jnp.float32),
            pltpu.VMEM((pieces, pairs, width), jnp.bfloat16),
            pltpu.VMEM(sent, jnp.bfloat16),
            pltpu.SemaphoreType.DMA((loads + 1,)),
            pltpu.SemaphoreType.DMA((pieces,)),
        ],
        compiler_params=pltpu.CompilerParams(vmem_limit_bytes=VMEM_LIMIT),
        cost_estimate=pl.CostEstimate(
            flops=2 * TEMP_ITERS * pairs * pairs * rows * columns, bytes_accessed=4 * 2**20, transcendentals=0
        ),
    )(flat, projector)
    misfit = misfit.reshape(pairs, tiles, rows, LANES).transpose(0, 2, 1, 3).reshape(pairs, rows, columns)
    return estimate, misfit


def deviation_kernel(above_ref, own_ref, below_ref, deviation_ref):
    def extended(at):
        return jnp.concatenate([ref[at] for ref in (above_ref, own_ref, below_ref)], axis=0).astype(jnp.float32)

    cycles_down, cycles_across, classes = extended(0), extended(1), extended(2)
    rows, columns = classes.shape
    limits = jnp.zeros(classes.shape, jnp.float32)
    for number, level in enumerate(LEVELS):
        limits = limits + jnp.where(classes == number + 1, level, 0.0)
    is_last = lax.broadcasted_iota(jnp.int32, classes.shape, 1) == columns - 1
    limits_across = jnp.where(is_last, 0.0, limits)
    limits_down = jnp.where(pltpu.roll(classes, rows - 1, 0) == 0, 0.0, limits)
    step_down, step_across = DUAL_STEP * cycles_down, DUAL_STEP * cycles_across
    shrink = 1.0 / (1.0 + PRIMAL_STEP * FIDELITY)

    zero = jnp.zeros(classes.shape, jnp.float32)
    deviation, deviation_bar, dual_down, dual_across = zero, zero, zero, zero
    for _ in range(SWEEPS):
        down = pltpu.roll(deviation_bar, rows - 1, 0) - deviation_bar
        across = pltpu.roll(deviation_bar, columns - 1, 1) - deviation_bar
        dual_down = clip(dual_down + DUAL_STEP * down - step_down, limits_down)
        dual_across = clip(dual_across + DUAL_STEP * across - step_across, limits_across)
        diverge = dual_down - pltpu.roll(dual_down, 1, 0) + dual_across - pltpu.roll(dual_across, 1, 1)
        updated = (deviation + PRIMAL_STEP * diverge) * shrink
        deviation_bar = 2.0 * updated - deviation
        deviation = updated
    deviation_ref[...] = deviation[HALO : HALO + deviation_ref.shape[0]]


def shifted(value, axis, by):
    peers = lax.axis_size(axis)
    pairs = [(i, i + by) for i in range(peers) if 0 <= i + by < peers]
    return lax.ppermute(value, axis, pairs)


def deviation_section(cycles_down, cycles_across, weight_class):
    own = jnp.stack([cycles_down, cycles_across, weight_class + 1])
    tiles = lax.axis_size("tile")
    tile = lax.axis_index("tile")
    even = tile % 2 == 0
    top, bottom = own[:, :HALO], own[:, -HALO:]
    inner = lax.ppermute(jnp.where(even, bottom, top), "tile", [(i, i ^ 1) for i in range(tiles)])
    outer = lax.ppermute(
        jnp.where(even, top, bottom), "tile", [(i, i - 1 if i % 2 == 0 else i + 1) for i in range(1, tiles - 1)]
    )
    above, below = jnp.where(even, outer, inner), jnp.where(even, inner, outer)
    in_vmem = pl.BlockSpec(memory_space=pltpu.VMEM)
    return pl.pallas_call(
        deviation_kernel,
        out_shape=jax.ShapeDtypeStruct(cycles_down.shape, jnp.float32),
        in_specs=[in_vmem] * 3,
        out_specs=in_vmem,
        compiler_params=pltpu.CompilerParams(vmem_limit_bytes=8 * 2**20),
        cost_estimate=pl.CostEstimate(flops=4 * 2**20, bytes_accessed=2**18, transcendentals=0),
    )(above, own, below)


def combine_kernel(order_ref, estimate_ref, deviation_ref, unwrapped_hbm, unwrapped_ref, sems):
    rows, pairs, columns = estimate_ref.shape
    group = order_ref.shape[0] // rows
    sent = []
    for at in range(pairs // group):
        part = pl.ds(at * group, group)
        turned = jnp.dot(
            order_ref[...],
            estimate_ref[:, part, :].reshape(rows * group, columns),
            preferred_element_type=jnp.float32,
        )
        unwrapped_ref[part] = turned.reshape(group, rows, columns) + deviation_ref[...][None]
        copy = pltpu.make_async_copy(unwrapped_ref.at[part], unwrapped_hbm.at[part], sems.at[at])
        copy.start()
        sent.append(copy)
    for copy in sent:
        copy.wait()


def combine(estimate, deviation):
    rows, pairs, columns = estimate.shape
    group = 16
    size = rows * group
    place = jnp.arange(size)
    source = place % rows * group + place // rows
    order = (source[:, None] == place[None]).astype(jnp.bfloat16)
    out = jax.ShapeDtypeStruct((pairs, rows, columns), jnp.float32)
    return pl.pallas_call(
        combine_kernel,
        out_shape=out,
        in_specs=[pl.BlockSpec(memory_space=pltpu.VMEM)] * 3,
        out_specs=pl.BlockSpec(memory_space=pl.ANY),
        scratch_shapes=[pltpu.VMEM(out.shape, out.dtype), pltpu.SemaphoreType.DMA((pairs // group,))],
        compiler_params=pltpu.CompilerParams(vmem_limit_bytes=16 * 2**20),
    )(order, estimate, deviation)


def per_device(wrapped, projector, cycles_down, cycles_across, weight_class):
    estimate, misfit = temporal_section(wrapped, projector, lax.axis_size("pair"))
    moved = lax.all_to_all(estimate, "pair", split_axis=0, concat_axis=0, tiled=True)
    deviation = deviation_section(cycles_down, cycles_across, weight_class)
    peers, rows, group, columns = moved.shape
    unwrapped = combine(moved.reshape(peers * rows, group, columns), deviation)
    return unwrapped, misfit


def solution(mesh):
    placed = (
        P(None, ("tile", "pair"), None),
        P(),
        P("tile", None),
        P("tile", None),
        P("tile", None),
    )
    return jax.shard_map(
        per_device,
        mesh=mesh,
        in_specs=placed,
        out_specs=(P("pair", "tile", None), P(None, ("tile", "pair"), None)),
        check_vma=False,
    )
```

```python
import functools

import jax
import jax.numpy as jnp
from jax import lax
from jax.experimental import pallas as pl
from jax.experimental.pallas import tpu as pltpu
from jax.sharding import PartitionSpec as P

TEMP_ITERS = 6
SWEEPS = 8


SHRINK = 0.5
DUAL_STEP = 0.35
PRIMAL_STEP = 0.35
FIDELITY = 0.5
LEVELS = (0.25, 0.5, 1.0, 2.0)

HALO = 8
LANES = 128
VMEM_LIMIT = 58 * 2**20


def clip(value, bound):
    return jnp.minimum(jnp.maximum(value, -bound), bound)


def temporal_kernel(
    wrapped_hbm,
    projector_hbm,
    estimate_hbm,
    excess_ref,
    wrapped_ref,
    projector_ref,
    spread_ref,
    phases_ref,
    multiplier_ref,
    blended_ref,
    estimate_ref,
    in_sems,
    out_sems,
):
    pairs = projector_ref.shape[0]
    per_pair = wrapped_ref.shape[0] // pairs
    peers, rows, group, _ = estimate_ref.shape
    pieces, _, width = multiplier_ref.shape
    wide = width // LANES
    loads = in_sems.shape[0] - 1
    load_rows = wrapped_ref.shape[0] // loads
    load_pairs = pairs // loads

    def parts_of(piece):
        return enumerate(range(piece * wide, (piece + 1) * wide))

    copies = []
    for load in range(loads):
        part = pl.ds(load * load_rows, load_rows)
        copies.append(pltpu.make_async_copy(wrapped_hbm.at[part], wrapped_ref.at[part], in_sems.at[load]))
    copies.append(pltpu.make_async_copy(projector_hbm, projector_ref, in_sems.at[loads]))
    for copy in copies:
        copy.start()
    for load in range(loads):
        copies[load].wait()
        first = load * load_rows
        spread_ref[first : first + load_rows, :] = wrapped_ref[first : first + load_rows, :].astype(jnp.float32)
        at_pairs = slice(load * load_pairs, (load + 1) * load_pairs)
        for piece in range(pieces):
            for at, k in parts_of(piece):
                columns = slice(at * LANES, (at + 1) * LANES)
                phases = spread_ref[pl.ds(first + k, load_pairs, stride=per_pair), :]
                phases_ref[piece, at_pairs, columns] = phases
                blended_ref[piece, at_pairs, columns] = phases.astype(jnp.bfloat16)
    copies[loads].wait()

    half = pairs // 2
    sent = []
    for iteration in range(TEMP_ITERS):
        for piece in range(pieces):
            blended, following = blended_ref[piece], []
            for begin in (0, half):
                part = slice(begin, begin + half)
                mapped = jnp.dot(projector_ref[part, :], blended, preferred_element_type=jnp.float32)
                carried = mapped if iteration == 0 else mapped + multiplier_ref[piece, part]
                excess = carried - phases_ref[piece, part]
                multiplier = clip(excess, SHRINK)
                if iteration < TEMP_ITERS - 1:
                    multiplier_ref[piece, part] = multiplier
                    following.append((carried - 2.0 * multiplier).astype(jnp.bfloat16))
                    continue
                excess_ref[piece, part] = excess
                estimate = mapped.astype(jnp.bfloat16)
                for at, k in parts_of(piece):
                    columns = slice(at * LANES, (at + 1) * LANES)
                    tile, row = divmod(k, rows)
                    for block in range(half // group):
                        estimate_ref[begin // group + block, row, :, tile * LANES : (tile + 1) * LANES] = estimate[
                            block * group : (block + 1) * group, columns
                        ]
            for begin, value in zip((0, half), following):
                blended_ref[piece, begin : begin + half] = value
            if iteration == TEMP_ITERS - 1:
                done = pl.ds(piece * width // rows, width // rows)
                copy = pltpu.make_async_copy(
                    estimate_ref.at[:, :, :, done], estimate_hbm.at[:, :, :, done], out_sems.at[piece]
                )
                copy.start()
                sent.append(copy)
    for copy in sent:
        copy.wait()


def misfit_kernel(excess_ref, misfit_hbm, misfit_ref, sem):
    pieces, pairs, width = excess_ref.shape
    wide = width // LANES
    for piece in range(pieces):
        excess = excess_ref[piece]
        misfit = excess - clip(excess, SHRINK)
        for at in range(wide):
            rows = pl.ds(piece * wide + at, pairs, stride=pieces * wide)
            misfit_ref[rows, :] = misfit[:, at * LANES : (at + 1) * LANES]
    copy = pltpu.make_async_copy(misfit_ref, misfit_hbm, sem)
    copy.start()
    copy.wait()


def temporal_section(wrapped, projector, peers):
    pairs, rows, columns = wrapped.shape
    tiles = columns // LANES
    flat = wrapped.reshape(pairs, rows, tiles, LANES).transpose(0, 2, 1, 3).reshape(-1, LANES)
    anywhere = pl.BlockSpec(memory_space=pl.ANY)
    width = 2 * LANES
    pieces = rows * columns // width
    loads = 4
    sent = (peers, rows, pairs // peers, columns)
    estimate, excess = pl.pallas_call(
        temporal_kernel,
        out_shape=(jax.ShapeDtypeStruct(sent, jnp.bfloat16), pltpu.VMEM((pieces, pairs, width), jnp.float32)),
        in_specs=[anywhere, anywhere],
        out_specs=(anywhere, pl.BlockSpec(memory_space=pltpu.VMEM)),
        scratch_shapes=[
            pltpu.VMEM(flat.shape, jnp.bfloat16),
            pltpu.VMEM(projector.shape, jnp.bfloat16),
            pltpu.VMEM(flat.shape, jnp.float32),
            pltpu.VMEM((pieces, pairs, width), jnp.float32),
            pltpu.VMEM((pieces, pairs, width), jnp.float32),
            pltpu.VMEM((pieces, pairs, width), jnp.bfloat16),
            pltpu.VMEM(sent, jnp.bfloat16),
            pltpu.SemaphoreType.DMA((loads + 1,)),
            pltpu.SemaphoreType.DMA((pieces,)),
        ],
        compiler_params=pltpu.CompilerParams(vmem_limit_bytes=VMEM_LIMIT),
        cost_estimate=pl.CostEstimate(
            flops=2 * TEMP_ITERS * pairs * pairs * rows * columns, bytes_accessed=4 * 2**20, transcendentals=0
        ),
    )(flat, projector)
    misfit = pl.pallas_call(
        misfit_kernel,
        out_shape=jax.ShapeDtypeStruct(flat.shape, jnp.float32),
        in_specs=[pl.BlockSpec(memory_space=pltpu.VMEM)],
        out_specs=anywhere,
        scratch_shapes=[pltpu.VMEM(flat.shape, jnp.float32), pltpu.SemaphoreType.DMA],
        compiler_params=pltpu.CompilerParams(vmem_limit_bytes=16 * 2**20),
        cost_estimate=pl.CostEstimate(flops=2**21, bytes_accessed=2**22, transcendentals=0),
    )(excess)
    misfit = misfit.reshape(pairs, tiles, rows, LANES).transpose(0, 2, 1, 3).reshape(pairs, rows, columns)
    return estimate, misfit


def deviation_kernel(above_ref, own_ref, below_ref, deviation_ref):
    def extended(at):
        return jnp.concatenate([ref[at] for ref in (above_ref, own_ref, below_ref)], axis=0).astype(jnp.float32)

    cycles_down, cycles_across, classes = extended(0), extended(1), extended(2)
    rows, columns = classes.shape
    limits = jnp.zeros(classes.shape, jnp.float32)
    for number, level in enumerate(LEVELS):
        limits = limits + jnp.where(classes == number + 1, level, 0.0)
    is_last = lax.broadcasted_iota(jnp.int32, classes.shape, 1) == columns - 1
    limits_across = jnp.where(is_last, 0.0, limits)
    limits_down = jnp.where(pltpu.roll(classes, rows - 1, 0) == 0, 0.0, limits)
    step_down, step_across = DUAL_STEP * cycles_down, DUAL_STEP * cycles_across
    shrink = 1.0 / (1.0 + PRIMAL_STEP * FIDELITY)

    zero = jnp.zeros(classes.shape, jnp.float32)
    deviation, deviation_bar, dual_down, dual_across = zero, zero, zero, zero
    for _ in range(SWEEPS):
        down = pltpu.roll(deviation_bar, rows - 1, 0) - deviation_bar
        across = pltpu.roll(deviation_bar, columns - 1, 1) - deviation_bar
        dual_down = clip(dual_down + DUAL_STEP * down - step_down, limits_down)
        dual_across = clip(dual_across + DUAL_STEP * across - step_across, limits_across)
        diverge = dual_down - pltpu.roll(dual_down, 1, 0) + dual_across - pltpu.roll(dual_across, 1, 1)
        updated = (deviation + PRIMAL_STEP * diverge) * shrink
        deviation_bar = 2.0 * updated - deviation
        deviation = updated
    deviation_ref[...] = deviation[HALO : HALO + deviation_ref.shape[0]]


def shifted(value, axis, by):
    peers = lax.axis_size(axis)
    pairs = [(i, i + by) for i in range(peers) if 0 <= i + by < peers]
    return lax.ppermute(value, axis, pairs)


def deviation_section(cycles_down, cycles_across, weight_class):
    own = jnp.stack([cycles_down, cycles_across, weight_class + 1])
    tiles = lax.axis_size("tile")
    tile = lax.axis_index("tile")
    even = tile % 2 == 0
    top, bottom = own[:, :HALO], own[:, -HALO:]
    inner = lax.ppermute(jnp.where(even, bottom, top), "tile", [(i, i ^ 1) for i in range(tiles)])
    outer = lax.ppermute(
        jnp.where(even, top, bottom), "tile", [(i, i - 1 if i % 2 == 0 else i + 1) for i in range(1, tiles - 1)]
    )
    above, below = jnp.where(even, outer, inner), jnp.where(even, inner, outer)
    in_vmem = pl.BlockSpec(memory_space=pltpu.VMEM)
    return pl.pallas_call(
        deviation_kernel,
        out_shape=jax.ShapeDtypeStruct(cycles_down.shape, jnp.float32),
        in_specs=[in_vmem] * 3,
        out_specs=in_vmem,
        compiler_params=pltpu.CompilerParams(vmem_limit_bytes=8 * 2**20),
        cost_estimate=pl.CostEstimate(flops=4 * 2**20, bytes_accessed=2**18, transcendentals=0),
    )(above, own, below)


def combine_kernel(order_ref, estimate_ref, deviation_ref, unwrapped_hbm, unwrapped_ref, sems):
    rows, pairs, columns = estimate_ref.shape
    group = order_ref.shape[0] // rows
    sent = []
    for at in range(pairs // group):
        part = pl.ds(at * group, group)
        turned = jnp.dot(
            order_ref[...],
            estimate_ref[:, part, :].reshape(rows * group, columns),
            preferred_element_type=jnp.float32,
        )
        unwrapped_ref[part] = turned.reshape(group, rows, columns) + deviation_ref[...][None]
        copy = pltpu.make_async_copy(unwrapped_ref.at[part], unwrapped_hbm.at[part], sems.at[at])
        copy.start()
        sent.append(copy)
    for copy in sent:
        copy.wait()


def combine(estimate, deviation):
    rows, pairs, columns = estimate.shape
    group = 16
    size = rows * group
    place = jnp.arange(size)
    source = place % rows * group + place // rows
    order = (source[:, None] == place[None]).astype(jnp.bfloat16)
    out = jax.ShapeDtypeStruct((pairs, rows, columns), jnp.float32)
    return pl.pallas_call(
        combine_kernel,
        out_shape=out,
        in_specs=[pl.BlockSpec(memory_space=pltpu.VMEM)] * 3,
        out_specs=pl.BlockSpec(memory_space=pl.ANY),
        scratch_shapes=[pltpu.VMEM(out.shape, out.dtype), pltpu.SemaphoreType.DMA((pairs // group,))],
        compiler_params=pltpu.CompilerParams(vmem_limit_bytes=16 * 2**20),
    )(order, estimate, deviation)


def per_device(wrapped, projector, cycles_down, cycles_across, weight_class):
    estimate, misfit = temporal_section(wrapped, projector, lax.axis_size("pair"))
    moved = lax.all_to_all(estimate, "pair", split_axis=0, concat_axis=0, tiled=True)
    deviation = deviation_section(cycles_down, cycles_across, weight_class)
    peers, rows, group, columns = moved.shape
    unwrapped = combine(moved.reshape(peers * rows, group, columns), deviation)
    return unwrapped, misfit


def solution(mesh):
    placed = (
        P(None, ("tile", "pair"), None),
        P(),
        P("tile", None),
        P("tile", None),
        P("tile", None),
    )
    return jax.shard_map(
        per_device,
        mesh=mesh,
        in_specs=placed,
        out_specs=(P("pair", "tile", None), P(None, ("tile", "pair"), None)),
        check_vma=False,
    )
```
